32 devices in a mesh: group: 2 (over x), row: 16 (over z, y, core).
Axes of the slice: x: 2, y: 2, z: 4, core: 2. Of those that a mesh axis runs over, the one named last changes fastest.
Arguments:
- base_currents: bfloat16 [32768, 1024], P(('group', 'row')), parts along dimension 0, may hold values from -6 to 6
- term_rows: bfloat16 [8192, 1024], P(('group', 'row')), parts along dimension 0, may hold values from -12 to 12
- term_owner: int32 [8192, 1], P(('group', 'row')), parts along dimension 0, may hold values from 0 to 15; in each aligned block of 256 rows (0 to 255, 256 to 511, ...) at most 32 rows name the same one
- term_slot: int32 [8192, 1], P(('group', 'row')), parts along dimension 0, may hold values from 0 to 1023
- inductance: bfloat16 [64, 20, 256, 256], P('row'), may hold values from -0.078125 to 0.078125
- block_cols: int32 [64, 20], P('row'), may hold values from 0 to 63, as said below
Outputs:
- flux: bfloat16 [32768, 1024], P(('group', 'row')), parts along dimension 0
The draws below stay inside these ranges and needn't reach their ends.
There are 2 independent parts, one for each index of `group`. The reference program is written for one: setup_inputs(seed, part) draws one part's arguments, and reference() takes and returns one part's arrays. A program takes and returns all parts, laid end to end along the dimension named above; an argument that names none is the same for every part. Nothing has to cross between parts.
Inputs may be any that keep to these rules, and one draw needn't show every extreme that they name: `block_cols`: the block rows of device i (block rows i * 4 to i * 4 + 3) list only block columns of devices i - 2 to i + 2; every block row lists a column of device max(i - 2, 0) and one of device min(i + 2, the last device). Columns may repeat. `term_owner`: among the 256 terminal rows of one device, at most 32 name the same owner, and that many is reached.
All inputs are finite; a program needn't handle non-finite values.
Results may differ from the reference program's by a relative error of at most 0.0046.
Values may be sent and summed in bfloat16 or wider, within the bound.
A program may use at most 128 MiB of HBM per device.

```python
import math
import jax
import jax.numpy as jnp
import numpy as np
from jax import lax

BLOCK = 256
RB_DEV = 4
K = 20
HALO = 2
W = 1024
TERM_DEV = 256
CAP = 32
SEG_DEV = 1024
ORDER = 16384
BROWS = 64
TERMS = 4096
N_ROW = 16


def draw_block_cols(key, part):
    devices = BROWS // RB_DEV
    row_ids = jnp.arange(BROWS)
    home_dev = row_ids // RB_DEV
    lowest = jnp.maximum(home_dev - HALO, 0)
    highest = jnp.minimum(home_dev + HALO, devices - 1)
    key_owner = jax.random.fold_in(key, 11)
    key_within = jax.random.fold_in(key, 12)
    key_forced = jax.random.fold_in(key, 13)
    owner_dev = jax.random.randint(key_owner, (BROWS, K), lowest[:, None], highest[:, None] + 1)
    forced = jax.random.randint(key_forced, (BROWS, 1), 0, K)
    entry_ids = jnp.arange(K)[None, :]
    owner_dev = jnp.where(entry_ids == forced, lowest[:, None], owner_dev)
    owner_dev = jnp.where(entry_ids == (forced + 1) % K, highest[:, None], owner_dev)
    within = jax.random.randint(key_within, (BROWS, K), 0, RB_DEV)
    return (owner_dev * RB_DEV + within).astype(jnp.int32)


def touch_ends(entries, rng, least, top_value):
    index_at = [jax.random.randint(jax.random.fold_in(rng, axis), (), 0, length) for axis, length in enumerate(entries.shape)]
    main_axis = entries.shape.index(max(entries.shape))
    next_to = index_at[:main_axis] + [(index_at[main_axis] + 1) % entries.shape[main_axis]] + index_at[main_axis + 1:]
    return entries.at[tuple(index_at)].set(least).at[tuple(next_to)].set(top_value)


def level_of(key, extent, cuts, least, largest):
    def one(axis_at, parts):
        steps = jax.random.uniform(jax.random.fold_in(jax.random.fold_in(key, 6), axis_at), (parts,), jnp.float32, least / len(cuts), largest / len(cuts))
        return jnp.repeat(jnp.exp(steps), extent[axis_at] // parts).reshape((-1,) + (1,) * (len(extent) - axis_at - 1))

    factor_of = one(*cuts[0])
    for cut in cuts[1:]:
        factor_of = factor_of * one(*cut)
    return factor_of


def routed_block(rng, own, number, rows, count, top, bound, lean):
    order = jax.random.permutation(rng, count)
    heavy_load, usual = portions_of(count, rows * top, bound, lean, True), portions_of(count, rows * top, bound, lean, False)
    places = jnp.arange(count)

    def named(lengths, rotation):
        used = int((lengths > 0).sum())
        fixed = max(1, used // 4)
        shifted = fixed + (places - fixed + rotation * (used - fixed)) % max(1, count - fixed)
        return jnp.zeros((count,), jnp.int32).at[order[jnp.where(places < fixed, places, shifted)]].set(jnp.asarray(lengths, jnp.int32))

    lengths = jnp.where(number % 4 == 0, named(heavy_load, number // 4), named(usual, number - number // 4 - 1))
    mixed = jax.random.permutation(jax.random.fold_in(own, 3), count)
    source_of, taker = mixed[0:count // 2 * 2:2], mixed[1:count // 2 * 2:2]
    margin = jnp.minimum(lengths[source_of] - 1, bound - lengths[taker]) // 2
    margin = jnp.where((source_of == order[0]) | (taker == order[0]) | (lengths[taker] == 0), 0, jnp.maximum(margin, 0))
    shifted = jax.random.randint(jax.random.fold_in(own, 4), (count // 2,), 0, 1 << 20) % (margin + 1)
    lengths = lengths.at[source_of].add(-shifted).at[taker].add(shifted)
    members = jnp.searchsorted(jnp.cumsum(lengths), jnp.arange(rows * top), side="right").astype(jnp.int32)
    grid = members.reshape(top, rows).T
    grid = grid[jax.random.permutation(jax.random.fold_in(own, 1), rows)]
    rotation = jax.random.randint(jax.random.fold_in(own, 2), (rows, 1), 0, top)
    return jnp.take_along_axis(grid, (jnp.arange(top)[None, :] + rotation) % top, axis=1)


def portions_of(number_of, total, bound, skew, full):
    loads = [(1 << 20) // math.isqrt(rank ** skew) + 1 for rank in range(1, number_of + 1)]
    largest = bound if full else min(bound, max(-(-total // number_of), total * loads[0] // sum(loads)))
    least = 1 if total - largest >= number_of - 1 else 0
    counts, spare = [largest] + [least] * (number_of - 1), total - largest - least * (number_of - 1)
    while spare > 0:
        free = [i for i in range(1, number_of) if counts[i] < largest] or [i for i in range(1, number_of) if counts[i] < bound]
        pool, budget = sum([loads[i] for i in free]), spare
        for i in free:
            addition = min(bound - counts[i], max(1, budget * loads[i] // pool), spare)
            counts[i] = counts[i] + addition
            spare = spare - addition
    return np.array(counts)


def bell_draw(key, dims, width, reach, shards=(), kind=jnp.bfloat16):
    array = width * jax.random.normal(key, dims, jnp.float32)
    if shards:
        array = array * level_of(key, dims, shards, -0.22, 0.18)
    return jnp.clip(array, -reach, reach).astype(kind)


def setup_inputs(seed: int = 0, part: int = 0) -> dict:
    splits = jax.random.split(jax.random.key(seed), 7)
    own_keys = jax.random.split(jax.random.fold_in(splits[6], part), 7)
    base_currents = bell_draw(own_keys[0], (ORDER, W), 1.0, 6.0, ((0, 16),))
    term_rows = bell_draw(own_keys[1], (TERMS, W), 3.0, 12.0, ((0, 16),))
    term_owner_keys = jax.random.split(jax.random.fold_in(own_keys[2], 1), TERMS // TERM_DEV)
    term_owner_turns = jax.random.permutation(jax.random.fold_in(own_keys[2], 3), TERMS // TERM_DEV)
    term_owner = jax.vmap(lambda own, number: routed_block(jax.random.fold_in(own_keys[2], 2), own, number, TERM_DEV, N_ROW, 1, CAP, 2))(term_owner_keys, term_owner_turns).reshape((TERMS, 1))
    term_slot = touch_ends(jax.random.randint(own_keys[3], (TERMS, 1), 0, SEG_DEV), jax.random.fold_in(own_keys[3], 1), 0, SEG_DEV - 1).astype(jnp.int32)
    inductance = bell_draw(splits[4], (BROWS, K, BLOCK, BLOCK), (K * BLOCK) ** -0.5, 0.078125, ((0, 16),))
    block_cols = draw_block_cols(jax.random.fold_in(splits[6], 71), part)
    return {"base_currents": base_currents, "term_rows": term_rows, "term_owner": term_owner, "term_slot": term_slot, "inductance": inductance, "block_cols": block_cols}


def reference(base_currents, term_rows, term_owner, term_slot, inductance, block_cols):
    segment_of = (term_owner[:, 0] * SEG_DEV + term_slot[:, 0]).astype(jnp.int32)
    injected = jax.ops.segment_sum(term_rows.astype(jnp.float32), segment_of, num_segments=ORDER)
    currents = (base_currents.astype(jnp.float32) + injected).astype(jnp.bfloat16)
    current_blocks = currents.reshape(BROWS, BLOCK, W)

    def one_row(inputs):
        tiles, columns = inputs
        picked = current_blocks[columns.astype(jnp.int32)]
        return jnp.einsum("kab,kbw->aw", tiles.astype(jnp.float32), picked.astype(jnp.float32))

    linked = lax.map(one_row, (inductance, block_cols))
    return linked.reshape(ORDER, W).astype(jnp.bfloat16)
```

```python
import functools

import jax
import jax.numpy as jnp
from jax import lax
from jax.experimental import pallas as pl
from jax.experimental.pallas import tpu as pltpu
from jax.sharding import PartitionSpec as P

WIDTHS = (1, 1, 2, 2, 2)
CHUNKS = len(WIDTHS)
LANES = 128
HALO = 2
MESH = pl.DeviceIdType.MESH
F32 = jnp.float32
BF16 = jnp.bfloat16
TO_Y, TO_Z, TO_CORE, TO_RELAY = range(4)
RELAYED = (1, 2)
AHEAD = 2


def kernel(n, cap, cols_hbm, owner_hbm, slot_hbm, terms_hbm, base_hbm, blocks_hbm, out_ref, *scratch):
    windows, scratch = scratch[:CHUNKS], scratch[CHUNKS:]
    outgoing, scratch = scratch[:CHUNKS], scratch[CHUNKS:]
    arrived, scratch = scratch[:CHUNKS], scratch[CHUNKS:]
    passing, scratch = scratch[:CHUNKS], scratch[CHUNKS:]
    (cols_ref, owner_ref, slot_ref, terms, base, blocks, landing, tags_out, tags_in,
     load_sem, own_sem, a2a_send, a2a_recv, pass_send, pass_recv, tag_sem, halo_send, halo_recv,
     piece_recv) = scratch
    me = lax.axis_index("row")
    count = terms.shape[0]
    seg_dev = base.shape[0]
    rows_dev, stored, block, _ = blocks.shape
    wides = [window.shape[2] for window in windows]
    starts = [sum(wides[:j]) for j in range(CHUNKS)]
    sign_c = 1 - 2 * (me % 2)
    sign_y = 1 - 2 * ((me // 2) % 2)
    z_to, z_from = me + 4 * sign_y, me - 4 * sign_y
    z_sends = jnp.logical_and(z_to >= 0, z_to < n)
    z_comes = jnp.logical_and(z_from >= 0, z_from < n)

    load_terms = pltpu.make_async_copy(terms_hbm, terms, load_sem.at[0])
    load_base = pltpu.make_async_copy(base_hbm, base, load_sem.at[1])
    load_blocks = pltpu.make_async_copy(blocks_hbm, blocks, load_sem.at[2])
    load_owner = pltpu.make_async_copy(owner_hbm, owner_ref, load_sem.at[3])
    load_slot = pltpu.make_async_copy(slot_hbm, slot_ref, load_sem.at[4])
    load_cols = pltpu.make_async_copy(cols_hbm, cols_ref, load_sem.at[5])
    for load in (load_owner, load_slot, load_terms, load_base, load_cols, load_blocks):
        load.start()

    barrier = pltpu.get_barrier_semaphore()

    @pl.loop(1, n)
    def _(step):
        pl.semaphore_signal(barrier, inc=1, device_id={"row": (me + step) % n}, device_id_type=MESH)

    load_owner.wait()
    owner = owner_ref[...]
    matches = (lax.broadcasted_iota(jnp.int32, (n, count), 0) == owner).astype(F32)
    before = lax.broadcasted_iota(jnp.int32, (count, count), 0) < lax.broadcasted_iota(jnp.int32, (count, count), 1)
    earlier = jnp.dot(matches.astype(BF16), before.astype(F32).astype(BF16), preferred_element_type=F32)
    order_in = jnp.sum(earlier * matches, axis=0, keepdims=True).astype(jnp.int32)
    position = ((owner // 2) % 2 * (n // 2) + owner // 4 * 2 + owner % 2) * cap + order_in
    picker = (lax.broadcasted_iota(jnp.int32, (n * cap, count), 0) == position).astype(F32).astype(BF16)

    def slot_of(device):
        return (device // 2) % 2 * (n // 2) + device // 4 * 2 + device % 2

    def tag_copy(peer, source):
        return pltpu.make_async_remote_copy(
            src_ref=tags_out.at[peer], dst_ref=tags_in.at[source], send_sem=tag_sem.at[0],
            recv_sem=tag_sem.at[1], device_id={"row": peer}, device_id_type=MESH)

    def row_copy(j, peer, source):
        return pltpu.make_async_remote_copy(
            src_ref=outgoing[j].at[slot_of(peer)], dst_ref=arrived[j].at[source], send_sem=a2a_send.at[j],
            recv_sem=a2a_recv.at[j], device_id={"row": peer}, device_id_type=MESH)

    def all_tags():
        others = pl.ds(0, n - 1)
        return pltpu.make_async_remote_copy(
            src_ref=tags_out.at[others], dst_ref=tags_in.at[others], send_sem=tag_sem.at[0],
            recv_sem=tag_sem.at[1], device_id={"row": (me + 1) % n}, device_id_type=MESH)

    def all_rows(j):
        others = pl.ds(0, n - 1)
        return pltpu.make_async_remote_copy(
            src_ref=outgoing[j].at[others], dst_ref=arrived[j].at[others], send_sem=a2a_send.at[j],
            recv_sem=a2a_recv.at[j], device_id={"row": (me + 1) % n}, device_id_type=MESH)

    own_tags = pltpu.make_async_copy(tags_out.at[me], tags_in.at[me], own_sem.at[CHUNKS])
    own_rows = [
        pltpu.make_async_copy(outgoing[j].at[slot_of(me)], arrived[j].at[me], own_sem.at[j]) for j in range(CHUNKS)
    ]

    def pack(j):
        sent = jnp.dot(picker, terms[:, starts[j]:starts[j] + wides[j]], preferred_element_type=F32)
        outgoing[j][...] = sent.astype(BF16).reshape(outgoing[j].shape)

    my_z, y_peer = me // 4, me + 2 * sign_y

    def over_y(j, hop):
        first = slot_of(me + 2 * sign_y + 4 * hop * sign_y - me % 2)
        return pltpu.make_async_remote_copy(
            src_ref=outgoing[j].at[pl.ds(first, 2)], dst_ref=passing[j].at[hop - 1], send_sem=a2a_send.at[j],
            recv_sem=pass_recv.at[j, hop - 1], device_id={"row": y_peer}, device_id_type=MESH)

    def over_z(j, hop, core):
        return pltpu.make_async_remote_copy(
            src_ref=passing[j].at[hop - 1, core], dst_ref=arrived[j].at[y_peer],
            send_sem=pass_send.at[j, hop - 1], recv_sem=a2a_recv.at[j],
            device_id={"row": me - me % 2 + core - 4 * hop * sign_y}, device_id_type=MESH)

    def passed(j, hop):
        return pltpu.make_async_remote_copy(
            src_ref=passing[j].at[hop - 1], dst_ref=passing[j].at[hop - 1], send_sem=pass_send.at[j, hop - 1],
            recv_sem=pass_recv.at[j, hop - 1], device_id={"row": y_peer}, device_id_type=MESH)

    def goes_over(hop):
        there = my_z + hop * sign_y
        return jnp.logical_and(there >= 0, there < n // 4)

    def comes_over(hop):
        there = my_z - hop * sign_y
        return jnp.logical_and(there >= 0, there < n // 4)

    def pass_rows(j):
        for hop in RELAYED:
            @pl.when(comes_over(hop))
            def _(hop=hop):
                passed(j, hop).wait_recv()
                for core in range(2):
                    over_z(j, hop, core).start()

    def send_over(j):
        for hop in reversed(RELAYED):
            @pl.when(goes_over(hop))
            def _(hop=hop):
                over_y(j, hop).start()

    def send_rows(j):
        @pl.loop(1, n)
        def _(step):
            peer = (me + step) % n
            hops = (peer // 4 - my_z) * sign_y
            other_y = (peer // 2) % 2 != (me // 2) % 2
            over = jnp.logical_and(other_y, jnp.logical_and(hops >= min(RELAYED, default=n), hops <= max(RELAYED, default=0)))

            @pl.when(jnp.logical_not(over))
            def _():
                row_copy(j, peer, me).start()

        own_rows[j].start()

    load_terms.wait()
    for j in range(CHUNKS):
        pack(j)
    per_row = LANES // cap
    lane_of = order_in + (me % per_row) * cap
    lanes = (lax.broadcasted_iota(jnp.int32, (LANES, count), 0) == lane_of).astype(F32).astype(BF16)
    load_slot.wait()
    tag = slot_ref[...] + 1
    high = (tag // 32).astype(F32)
    low = (tag % 32).astype(F32)
    over_rows = (((1,), (1,)), ((), ()))
    tags = 32.0 * lax.dot_general((matches * high).astype(BF16), lanes, over_rows, preferred_element_type=F32)
    tags = tags + lax.dot_general((matches * low).astype(BF16), lanes, over_rows, preferred_element_type=F32)
    tags = tags.astype(jnp.int32)
    for peer in range(n):
        tags_out[peer] = jnp.broadcast_to(tags[peer:peer + 1], tags_out.shape[1:])

    pl.semaphore_wait(barrier, n - 1)
    send_over(0)
    send_rows(0)

    @pl.loop(1, n)
    def _(step):
        tag_copy((me + step) % n, me).start()

    own_tags.start()
    pass_rows(0)
    for j in range(1, CHUNKS):
        send_over(j)

    all_tags().wait_recv()
    own_tags.wait()
    packed = []
    for first in range(0, n, per_row):
        total = tags_in[first][0:1]
        for source in range(first + 1, min(first + per_row, n)):
            total = total + tags_in[source][0:1]
        packed.append(total)
    arrived_tags = jnp.concatenate(packed, axis=1) - 1
    tall = seg_dev // 4
    for part in range(4):
        seg_ids = lax.broadcasted_iota(jnp.int32, (tall, n * cap), 0) + part * tall
        landing[part * tall:(part + 1) * tall] = (seg_ids == arrived_tags).astype(F32).astype(BF16)
    load_base.wait()

    def halo_copy(kind, j, from_slot, to_slot, peer):
        return pltpu.make_async_remote_copy(
            src_ref=windows[j].at[pl.ds(rows_dev * from_slot, rows_dev)],
            dst_ref=windows[j].at[pl.ds(rows_dev * to_slot, rows_dev)],
            send_sem=halo_send.at[kind, j], recv_sem=halo_recv.at[kind, j],
            device_id={"row": peer}, device_id_type=MESH)

    def piece_copy(kind, p, from_slot, to_slot, peer):
        j, q = divmod(p, rows_dev)
        recv_sem = halo_recv.at[kind, j] if kind == TO_RELAY else piece_recv.at[kind, p]
        return pltpu.make_async_remote_copy(
            src_ref=windows[j].at[rows_dev * from_slot + q], dst_ref=windows[j].at[rows_dev * to_slot + q],
            send_sem=halo_send.at[kind, j], recv_sem=recv_sem, device_id={"row": peer}, device_id_type=MESH)

    y_way = (HALO, HALO - 2 * sign_y, me + 2 * sign_y)
    core_way = (HALO, HALO - sign_c, me + sign_c)
    z_way = (HALO + 2 * sign_y, HALO - 2 * sign_y, z_to)
    relay_way = (HALO + 2 * sign_c, HALO + sign_c, me + sign_c)
    relay_sends = jnp.logical_or(sign_y == sign_c, z_comes)
    relay_comes = jnp.logical_or(sign_y != sign_c, z_comes)
    first_block = (me - HALO) * rows_dev
    pieces = CHUNKS * rows_dev

    def own(j):
        all_rows(j).wait_recv()
        own_rows[j].wait()
        if j + 1 < CHUNKS:
            send_rows(j + 1)
            pass_rows(j + 1)
        rows = arrived[j][...].reshape(n * cap, wides[j])
        for q in range(rows_dev):
            place = slice(q * block, (q + 1) * block)
            injected = jnp.dot(landing[place], rows, preferred_element_type=F32)
            before_it = base[place, starts[j]:starts[j] + wides[j]].astype(F32)
            windows[j][HALO * rows_dev + q] = (before_it + injected).astype(BF16)
            piece_copy(TO_Y, j * rows_dev + q, *y_way).start()
        halo_copy(TO_CORE, j, *core_way).start()

    def y_arrives(p):
        slot = HALO + 2 * sign_y
        piece_copy(TO_Y, p, slot, slot, me + 2 * sign_y).wait_recv()

        @pl.when(z_sends)
        def _():
            piece_copy(TO_Z, p, *z_way).start()

        @pl.when(sign_y == sign_c)
        def _():
            piece_copy(TO_RELAY, p, *relay_way).start()

    def z_arrives(p):
        slot = HALO - 2 * sign_y

        @pl.when(z_comes)
        def _():
            piece_copy(TO_Z, p, slot, slot, me + 2 * sign_y).wait_recv()

        @pl.when(jnp.logical_and(z_comes, sign_y != sign_c))
        def _():
            piece_copy(TO_RELAY, p, *relay_way).start()

    def window_complete(j):
        halo_copy(TO_CORE, j, HALO + sign_c, HALO + sign_c, me + sign_c).wait_recv()

        @pl.when(relay_comes)
        def _():
            halo_copy(TO_RELAY, j, HALO - sign_c, HALO - sign_c, me + sign_c).wait_recv()

    def compute(j, r):
        total = jnp.zeros((block, wides[j]), F32)
        for k in range(stored):
            place = jnp.clip(cols_ref[r, k] - first_block, 0, windows[j].shape[0] - 1)
            total = total + jnp.dot(blocks[r, k], windows[j][place], preferred_element_type=F32)
        out_ref[r * block:(r + 1) * block, starts[j]:starts[j] + wides[j]] = total.astype(BF16)

    own(0)
    z_lag, lag = 2, rows_dev + 2
    for p in range(pieces + lag):
        if p < pieces:
            y_arrives(p)
            if p % rows_dev == rows_dev - 1 - AHEAD and p // rows_dev + 1 < CHUNKS:
                own(p // rows_dev + 1)
        if 0 <= p - z_lag < pieces:
            z_arrives(p - z_lag)
        if p == lag:
            load_cols.wait()
            load_blocks.wait()
        if p >= lag:
            j, r = divmod(p - lag, rows_dev)
            if r == 0:
                window_complete(j)
            compute(j, r)

    all_tags().wait_send()
    for j in range(CHUNKS):
        all_rows(j).wait_send()
        halo_copy(TO_Y, j, *y_way).wait_send()
        halo_copy(TO_CORE, j, *core_way).wait_send()

        @pl.when(z_sends)
        def _():
            halo_copy(TO_Z, j, *z_way).wait_send()

        @pl.when(relay_sends)
        def _():
            halo_copy(TO_RELAY, j, *relay_way).wait_send()

        for hop in RELAYED:
            @pl.when(comes_over(hop))
            def _(hop=hop):
                passed(j, hop).wait_send()


def shards(base_currents, term_rows, term_owner, term_slot, inductance, block_cols):
    n = lax.axis_size("row")
    seg_dev, width = base_currents.shape
    count = term_rows.shape[0]
    rows_dev, stored, block, _ = inductance.shape
    cap = max(16, 2 * count // n)
    wides = [width * part // sum(WIDTHS) for part in WIDTHS]
    span = (2 * HALO + 1) * rows_dev
    hbm = pl.BlockSpec(memory_space=pltpu.HBM)
    dma = pltpu.SemaphoreType.DMA
    return pl.pallas_call(
        functools.partial(kernel, n, cap),
        out_shape=pltpu.VMEM((seg_dev, width), BF16),
        in_specs=[hbm] * 6,
        out_specs=pl.BlockSpec(memory_space=pltpu.VMEM),
        scratch_shapes=(
            [pltpu.VMEM((span, block, wide), BF16) for wide in wides]
            + [pltpu.VMEM((n, cap, wide), BF16) for wide in wides]
            + [pltpu.VMEM((n, cap, wide), BF16) for wide in wides]
            + [pltpu.VMEM((max(RELAYED, default=1), 2, cap, wide), BF16) for wide in wides]
            + [
                pltpu.SMEM(block_cols.shape, jnp.int32),
                pltpu.VMEM((1, count), jnp.int32),
                pltpu.VMEM((1, count), jnp.int32),
                pltpu.VMEM((count, width), BF16),
                pltpu.VMEM((seg_dev, width), BF16),
                pltpu.VMEM(inductance.shape, BF16),
                pltpu.VMEM((seg_dev, n * cap), BF16),
                pltpu.VMEM((n, 8, LANES), jnp.int32),
                pltpu.VMEM((n, 8, LANES), jnp.int32),
                dma((6,)),
                dma((CHUNKS + 1,)),
                dma((CHUNKS,)),
                dma((CHUNKS,)),
                dma((CHUNKS, max(RELAYED, default=1))),
                dma((CHUNKS, max(RELAYED, default=1))),
                dma((2,)),
                dma((4, CHUNKS)),
                dma((4, CHUNKS)),
                dma((2, CHUNKS * rows_dev)),
            ]
        ),
        compiler_params=pltpu.CompilerParams(
            collective_id=0, has_side_effects=True, vmem_limit_bytes=48 * 2**20
        ),
        cost_estimate=pl.CostEstimate(
            flops=2 * rows_dev * stored * block * block * width,
            bytes_accessed=2 * (inductance.size + 2 * base_currents.size + term_rows.size),
            transcendentals=0,
        ),
    )(*[
        pltpu.with_memory_space_constraint(array, pltpu.HBM)
        for array in (
            block_cols, term_owner.reshape(1, count), term_slot.reshape(1, count), term_rows, base_currents, inductance
        )
    ])


def solution(mesh):
    placed = (
        P(("group", "row"), None),
        P(("group", "row"), None),
        P(("group", "row"), None),
        P(("group", "row"), None),
        P("row", None, None, None),
        P("row", None),
    )
    return jax.shard_map(
        shards, mesh=mesh, in_specs=placed, out_specs=P(("group", "row"), None), check_vma=False
    )
```

```python
import functools

import jax
import jax.numpy as jnp
from jax import lax
from jax.experimental import pallas as pl
from jax.experimental.pallas import tpu as pltpu
from jax.sharding import PartitionSpec as P

WIDTHS = (1, 1, 2, 2, 2)
CHUNKS = len(WIDTHS)
LANES = 128
HALO = 2
MESH = pl.DeviceIdType.MESH
F32 = jnp.float32
BF16 = jnp.bfloat16
TO_Y, TO_Z, TO_CORE, TO_RELAY = range(4)
RELAYED = ((), (), (1, 2), (1, 2), (1, 2))
DEPTH = 4
EARLY = 0
EDGE = False
LAGS = (5, 5, 6, 6)
SENDS = ((0,), (1, 2), (3,), (4,))


def kernel(n, cap, cols_hbm, owner_hbm, slot_hbm, terms_hbm, base_hbm, blocks_hbm, out_ref, *scratch):
    windows, scratch = scratch[:CHUNKS], scratch[CHUNKS:]
    outgoing, scratch = scratch[:CHUNKS], scratch[CHUNKS:]
    arrived, scratch = scratch[:CHUNKS], scratch[CHUNKS:]
    passing, scratch = scratch[:CHUNKS], scratch[CHUNKS:]
    (cols_ref, owner_ref, slot_ref, terms, base, blocks, landing, tags_out, tags_in,
     load_sem, own_sem, a2a_send, a2a_recv, pass_send, pass_recv, tag_sem, halo_send, halo_recv,
     piece_recv) = scratch
    me = lax.axis_index("row")
    count = terms.shape[0]
    seg_dev = base.shape[0]
    rows_dev, stored, block, _ = blocks.shape
    wides = [window.shape[2] for window in windows]
    starts = [sum(wides[:j]) for j in range(CHUNKS)]
    sign_c = 1 - 2 * (me % 2)
    sign_y = 1 - 2 * ((me // 2) % 2)
    z_to, z_from = me + 4 * sign_y, me - 4 * sign_y
    z_sends = jnp.logical_and(z_to >= 0, z_to < n)
    z_comes = jnp.logical_and(z_from >= 0, z_from < n)

    load_terms = pltpu.make_async_copy(terms_hbm, terms, load_sem.at[0])
    load_base = pltpu.make_async_copy(base_hbm, base, load_sem.at[1])
    load_blocks = pltpu.make_async_copy(blocks_hbm, blocks, load_sem.at[2])
    load_owner = pltpu.make_async_copy(owner_hbm, owner_ref, load_sem.at[3])
    load_slot = pltpu.make_async_copy(slot_hbm, slot_ref, load_sem.at[4])
    load_cols = pltpu.make_async_copy(cols_hbm, cols_ref, load_sem.at[5])
    for load in (load_owner, load_slot, load_terms, load_base, load_cols, load_blocks):
        load.start()

    barrier = pltpu.get_barrier_semaphore()

    @pl.loop(1, n)
    def _(step):
        pl.semaphore_signal(barrier, inc=1, device_id={"row": (me + step) % n}, device_id_type=MESH)

    load_owner.wait()
    owner = owner_ref[...]
    matches = (lax.broadcasted_iota(jnp.int32, (n, count), 0) == owner).astype(F32)
    before = lax.broadcasted_iota(jnp.int32, (count, count), 0) < lax.broadcasted_iota(jnp.int32, (count, count), 1)
    earlier = jnp.dot(matches.astype(BF16), before.astype(F32).astype(BF16), preferred_element_type=F32)
    order_in = jnp.sum(earlier * matches, axis=0, keepdims=True).astype(jnp.int32)
    position = ((owner // 2) % 2 * (n // 2) + owner // 4 * 2 + owner % 2) * cap + order_in
    picker = (lax.broadcasted_iota(jnp.int32, (n * cap, count), 0) == position).astype(F32).astype(BF16)

    def slot_of(device):
        return (device // 2) % 2 * (n // 2) + device // 4 * 2 + device % 2

    def tag_copy(peer, source):
        return pltpu.make_async_remote_copy(
            src_ref=tags_out.at[peer], dst_ref=tags_in.at[source], send_sem=tag_sem.at[0],
            recv_sem=tag_sem.at[1], device_id={"row": peer}, device_id_type=MESH)

    def row_copy(j, peer, source):
        return pltpu.make_async_remote_copy(
            src_ref=outgoing[j].at[slot_of(peer)], dst_ref=arrived[j].at[source], send_sem=a2a_send.at[j],
            recv_sem=a2a_recv.at[j], device_id={"row": peer}, device_id_type=MESH)

    def all_tags():
        others = pl.ds(0, n - 1)
        return pltpu.make_async_remote_copy(
            src_ref=tags_out.at[others], dst_ref=tags_in.at[others], send_sem=tag_sem.at[0],
            recv_sem=tag_sem.at[1], device_id={"row": (me + 1) % n}, device_id_type=MESH)

    def all_rows(j):
        others = pl.ds(0, n - 1)
        return pltpu.make_async_remote_copy(
            src_ref=outgoing[j].at[others], dst_ref=arrived[j].at[others], send_sem=a2a_send.at[j],
            recv_sem=a2a_recv.at[j], device_id={"row": (me + 1) % n}, device_id_type=MESH)

    own_tags = pltpu.make_async_copy(tags_out.at[me], tags_in.at[me], own_sem.at[CHUNKS])
    own_rows = [
        pltpu.make_async_copy(outgoing[j].at[slot_of(me)], arrived[j].at[me], own_sem.at[j]) for j in range(CHUNKS)
    ]

    def pack(j):
        sent = jnp.dot(picker, terms[:, starts[j]:starts[j] + wides[j]], preferred_element_type=F32)
        outgoing[j][...] = sent.astype(BF16).reshape(outgoing[j].shape)

    my_z, y_peer = me // 4, me + 2 * sign_y

    def over_y(j, hop):
        first = slot_of(me + 2 * sign_y + 4 * hop * sign_y - me % 2)
        return pltpu.make_async_remote_copy(
            src_ref=outgoing[j].at[pl.ds(first, 2)], dst_ref=passing[j].at[hop - 1], send_sem=a2a_send.at[j],
            recv_sem=pass_recv.at[j, hop - 1], device_id={"row": y_peer}, device_id_type=MESH)

    def over_z(j, hop, core):
        return pltpu.make_async_remote_copy(
            src_ref=passing[j].at[hop - 1, core], dst_ref=arrived[j].at[y_peer],
            send_sem=pass_send.at[j, hop - 1], recv_sem=a2a_recv.at[j],
            device_id={"row": me - me % 2 + core - 4 * hop * sign_y}, device_id_type=MESH)

    def passed(j, hop):
        return pltpu.make_async_remote_copy(
            src_ref=passing[j].at[hop - 1], dst_ref=passing[j].at[hop - 1], send_sem=pass_send.at[j, hop - 1],
            recv_sem=pass_recv.at[j, hop - 1], device_id={"row": y_peer}, device_id_type=MESH)

    def plane(there):
        return jnp.logical_and(there >= 0, there < n // 4)

    def straight(hop, behind):
        return jnp.logical_and(EDGE and hop == 2, jnp.logical_and(me % 2 == 1, jnp.logical_not(plane(behind))))

    def goes_over(hop):
        return jnp.logical_and(plane(my_z + hop * sign_y), jnp.logical_not(straight(hop, my_z - sign_y)))

    def comes_over(hop):
        return jnp.logical_and(plane(my_z - hop * sign_y), jnp.logical_not(straight(hop, my_z + sign_y)))

    def pass_rows(j):
        for hop in RELAYED[j]:
            @pl.when(comes_over(hop))
            def _(hop=hop):
                passed(j, hop).wait_recv()
                for core in range(2):
                    over_z(j, hop, core).start()

    def send_over(j):
        for hop in reversed(RELAYED[j]):
            @pl.when(goes_over(hop))
            def _(hop=hop):
                over_y(j, hop).start()

    def send_rows(j):
        @pl.loop(1, n)
        def _(step):
            peer = (me + step) % n
            hops = (peer // 4 - my_z) * sign_y
            other_y = (peer // 2) % 2 != (me // 2) % 2
            over = jnp.bool_(False)
            for hop in RELAYED[j]:
                over = jnp.logical_or(over, jnp.logical_and(hops == hop, goes_over(hop)))
            over = jnp.logical_and(other_y, over)

            @pl.when(jnp.logical_not(over))
            def _():
                row_copy(j, peer, me).start()

        own_rows[j].start()

    load_terms.wait()
    for j in range(CHUNKS):
        pack(j)
    per_row = LANES // cap
    lane_of = order_in + (me % per_row) * cap
    lanes = (lax.broadcasted_iota(jnp.int32, (LANES, count), 0) == lane_of).astype(F32).astype(BF16)
    load_slot.wait()
    tag = slot_ref[...] + 1
    high = (tag // 32).astype(F32)
    low = (tag % 32).astype(F32)
    over_rows = (((1,), (1,)), ((), ()))
    tags = 32.0 * lax.dot_general((matches * high).astype(BF16), lanes, over_rows, preferred_element_type=F32)
    tags = tags + lax.dot_general((matches * low).astype(BF16), lanes, over_rows, preferred_element_type=F32)
    tags = tags.astype(jnp.int32)
    for peer in range(n):
        tags_out[peer] = jnp.broadcast_to(tags[peer:peer + 1], tags_out.shape[1:])

    pl.semaphore_wait(barrier, n - 1)
    for j in SENDS[0]:
        send_over(j)
        send_rows(j)

    @pl.loop(1, n)
    def _(step):
        tag_copy((me + step) % n, me).start()

    own_tags.start()
    for j in SENDS[0]:
        pass_rows(j)
    for j in range(CHUNKS):
        if j not in SENDS[0]:
            send_over(j)

    all_tags().wait_recv()
    own_tags.wait()
    packed = []
    for first in range(0, n, per_row):
        total = tags_in[first][0:1]
        for source in range(first + 1, min(first + per_row, n)):
            total = total + tags_in[source][0:1]
        packed.append(total)
    arrived_tags = jnp.concatenate(packed, axis=1) - 1
    tall = seg_dev // 4
    for part in range(4):
        seg_ids = lax.broadcasted_iota(jnp.int32, (tall, n * cap), 0) + part * tall
        landing[part * tall:(part + 1) * tall] = (seg_ids == arrived_tags).astype(F32).astype(BF16)
    load_base.wait()

    def halo_copy(kind, j, from_slot, to_slot, peer):
        return pltpu.make_async_remote_copy(
            src_ref=windows[j].at[pl.ds(rows_dev * from_slot, rows_dev)],
            dst_ref=windows[j].at[pl.ds(rows_dev * to_slot, rows_dev)],
            send_sem=halo_send.at[kind, j], recv_sem=halo_recv.at[kind, j],
            device_id={"row": peer}, device_id_type=MESH)

    def piece_copy(kind, p, from_slot, to_slot, peer):
        j, q = divmod(p, rows_dev)
        recv_sem = halo_recv.at[kind, j] if kind == TO_RELAY else piece_recv.at[kind, p]
        return pltpu.make_async_remote_copy(
            src_ref=windows[j].at[rows_dev * from_slot + q], dst_ref=windows[j].at[rows_dev * to_slot + q],
            send_sem=halo_send.at[kind, j], recv_sem=recv_sem, device_id={"row": peer}, device_id_type=MESH)

    y_way = (HALO, HALO - 2 * sign_y, me + 2 * sign_y)
    core_way = (HALO, HALO - sign_c, me + sign_c)
    z_way = (HALO + 2 * sign_y, HALO - 2 * sign_y, z_to)
    relay_way = (HALO + 2 * sign_c, HALO + sign_c, me + sign_c)
    relay_sends = jnp.logical_or(sign_y == sign_c, z_comes)
    relay_comes = jnp.logical_or(sign_y != sign_c, z_comes)
    first_block = (me - HALO) * rows_dev
    pieces = CHUNKS * rows_dev

    def own(j):
        all_rows(j).wait_recv()
        own_rows[j].wait()
        for i in SENDS[j + 1] if j + 1 < len(SENDS) else ():
            send_rows(i)
            pass_rows(i)
        rows = arrived[j][...].reshape(n * cap, wides[j])
        for q in range(rows_dev):
            place = slice(q * block, (q + 1) * block)
            injected = jnp.dot(landing[place], rows, preferred_element_type=F32)
            before_it = base[place, starts[j]:starts[j] + wides[j]].astype(F32)
            windows[j][HALO * rows_dev + q] = (before_it + injected).astype(BF16)
        halo_copy(TO_CORE, j, *core_way).start()

    def y_arrives(p):
        slot = HALO + 2 * sign_y
        piece_copy(TO_Y, p, slot, slot, me + 2 * sign_y).wait_recv()

        @pl.when(z_sends)
        def _():
            piece_copy(TO_Z, p, *z_way).start()

        @pl.when(sign_y == sign_c)
        def _():
            piece_copy(TO_RELAY, p, *relay_way).start()

    def z_arrives(p):
        slot = HALO - 2 * sign_y

        @pl.when(z_comes)
        def _():
            piece_copy(TO_Z, p, slot, slot, me + 2 * sign_y).wait_recv()

        @pl.when(jnp.logical_and(z_comes, sign_y != sign_c))
        def _():
            piece_copy(TO_RELAY, p, *relay_way).start()

    def window_complete(j):
        halo_copy(TO_CORE, j, HALO + sign_c, HALO + sign_c, me + sign_c).wait_recv()

        @pl.when(relay_comes)
        def _():
            halo_copy(TO_RELAY, j, HALO - sign_c, HALO - sign_c, me + sign_c).wait_recv()

    def compute(j, r):
        total = jnp.zeros((block, wides[j]), F32)
        for k in range(stored):
            place = jnp.clip(cols_ref[r, k] - first_block, 0, windows[j].shape[0] - 1)
            total = total + jnp.dot(blocks[r, k], windows[j][place], preferred_element_type=F32)
        out_ref[r * block:(r + 1) * block, starts[j]:starts[j] + wides[j]] = total.astype(BF16)

    own(0)
    for p in range(DEPTH):
        if p > 0 and p % rows_dev == 0:
            own(p // rows_dev)
        piece_copy(TO_Y, p, *y_way).start()
    for p in range(DEPTH, DEPTH + EARLY):
        if p % rows_dev == 0:
            own(p // rows_dev)
    z_lag = 2
    first_compute = min(LAGS)
    for p in range(pieces - rows_dev + max(LAGS) + 1):
        if p < pieces:
            y_arrives(p)
            if p + DEPTH < pieces:
                if (p + DEPTH) // rows_dev > 0 and (p + DEPTH) % rows_dev == 0 and not EARLY:
                    own((p + DEPTH) // rows_dev)
                piece_copy(TO_Y, p + DEPTH, *y_way).start()
            ready = p + DEPTH + EARLY
            if EARLY and ready % rows_dev == 0 and 0 < ready // rows_dev < CHUNKS:
                own(ready // rows_dev)
        if 0 <= p - z_lag < pieces:
            z_arrives(p - z_lag)
        if p == first_compute:
            load_cols.wait()
            load_blocks.wait()
        for j in range(CHUNKS):
            for r in range(rows_dev):
                if p == rows_dev * j + LAGS[r % len(LAGS)]:
                    if r == 0:
                        window_complete(j)
                    compute(j, r)

    all_tags().wait_send()
    for j in range(CHUNKS):
        all_rows(j).wait_send()
        halo_copy(TO_Y, j, *y_way).wait_send()
        halo_copy(TO_CORE, j, *core_way).wait_send()

        @pl.when(z_sends)
        def _():
            halo_copy(TO_Z, j, *z_way).wait_send()

        @pl.when(relay_sends)
        def _():
            halo_copy(TO_RELAY, j, *relay_way).wait_send()

        for hop in RELAYED[j]:
            @pl.when(comes_over(hop))
            def _(hop=hop):
                passed(j, hop).wait_send()


def shards(base_currents, term_rows, term_owner, term_slot, inductance, block_cols):
    n = lax.axis_size("row")
    seg_dev, width = base_currents.shape
    count = term_rows.shape[0]
    rows_dev, stored, block, _ = inductance.shape
    cap = max(16, 2 * count // n)
    wides = [width * part // sum(WIDTHS) for part in WIDTHS]
    span = (2 * HALO + 1) * rows_dev
    hbm = pl.BlockSpec(memory_space=pltpu.HBM)
    dma = pltpu.SemaphoreType.DMA
    return pl.pallas_call(
        functools.partial(kernel, n, cap),
        out_shape=pltpu.VMEM((seg_dev, width), BF16),
        in_specs=[hbm] * 6,
        out_specs=pl.BlockSpec(memory_space=pltpu.VMEM),
        scratch_shapes=(
            [pltpu.VMEM((span, block, wide), BF16) for wide in wides]
            + [pltpu.VMEM((n, cap, wide), BF16) for wide in wides]
            + [pltpu.VMEM((n, cap, wide), BF16) for wide in wides]
            + [pltpu.VMEM((2, 2, cap, wide), BF16) for wide in wides]
            + [
                pltpu.SMEM(block_cols.shape, jnp.int32),
                pltpu.VMEM((1, count), jnp.int32),
                pltpu.VMEM((1, count), jnp.int32),
                pltpu.VMEM((count, width), BF16),
                pltpu.VMEM((seg_dev, width), BF16),
                pltpu.VMEM(inductance.shape, BF16),
                pltpu.VMEM((seg_dev, n * cap), BF16),
                pltpu.VMEM((n, 8, LANES), jnp.int32),
                pltpu.VMEM((n, 8, LANES), jnp.int32),
                dma((6,)),
                dma((CHUNKS + 1,)),
                dma((CHUNKS,)),
                dma((CHUNKS,)),
                dma((CHUNKS, 2)),
                dma((CHUNKS, 2)),
                dma((2,)),
                dma((4, CHUNKS)),
                dma((4, CHUNKS)),
                dma((2, CHUNKS * rows_dev)),
            ]
        ),
        compiler_params=pltpu.CompilerParams(
            collective_id=0, has_side_effects=True, vmem_limit_bytes=48 * 2**20
        ),
        cost_estimate=pl.CostEstimate(
            flops=2 * rows_dev * stored * block * block * width,
            bytes_accessed=2 * (inductance.size + 2 * base_currents.size + term_rows.size),
            transcendentals=0,
        ),
    )(*[
        pltpu.with_memory_space_constraint(array, pltpu.HBM)
        for array in (
            block_cols, term_owner.reshape(1, count), term_slot.reshape(1, count), term_rows, base_currents, inductance
        )
    ])


def solution(mesh):
    placed = (
        P(("group", "row"), None),
        P(("group", "row"), None),
        P(("group", "row"), None),
        P(("group", "row"), None),
        P("row", None, None, None),
        P("row", None),
    )
    return jax.shard_map(
        shards, mesh=mesh, in_specs=placed, out_specs=P(("group", "row"), None), check_vma=False
    )
```

```python
import functools

import jax
import jax.numpy as jnp
from jax import lax
from jax.experimental import pallas as pl
from jax.experimental.pallas import tpu as pltpu
from jax.sharding import PartitionSpec as P

WIDTHS = (1, 1, 2, 2, 2)
CHUNKS = len(WIDTHS)
LANES = 128
HALO = 2
MESH = pl.DeviceIdType.MESH
F32 = jnp.float32
BF16 = jnp.bfloat16
TO_Y, TO_Z, TO_CORE, TO_RELAY = range(4)
RELAYED = ((), (), (1, 2), (1, 2), (1, 2))
DEPTHS = (4, 4, 4, 4, 4)
Z_LAG = 2
EDGE = False
LAGS = (5, 5, 6, 6)
SENDS = ((0,), (1, 2), (), (3,), (4,))


def kernel(n, cap, cols_hbm, owner_hbm, slot_hbm, terms_hbm, base_hbm, blocks_hbm, out_ref, *scratch):
    windows, scratch = scratch[:CHUNKS], scratch[CHUNKS:]
    outgoing, scratch = scratch[:CHUNKS], scratch[CHUNKS:]
    arrived, scratch = scratch[:CHUNKS], scratch[CHUNKS:]
    passing, scratch = scratch[:CHUNKS], scratch[CHUNKS:]
    (cols_ref, owner_ref, slot_ref, terms, base, blocks, landing, tags_out, tags_in,
     load_sem, own_sem, a2a_send, a2a_recv, pass_send, pass_recv, tag_sem, halo_send, halo_recv,
     piece_recv) = scratch
    me = lax.axis_index("row")
    count = terms.shape[0]
    seg_dev = base.shape[0]
    rows_dev, stored, block, _ = blocks.shape
    wides = [window.shape[2] for window in windows]
    starts = [sum(wides[:j]) for j in range(CHUNKS)]
    sign_c = 1 - 2 * (me % 2)
    sign_y = 1 - 2 * ((me // 2) % 2)
    z_to, z_from = me + 4 * sign_y, me - 4 * sign_y
    z_sends = jnp.logical_and(z_to >= 0, z_to < n)
    z_comes = jnp.logical_and(z_from >= 0, z_from < n)

    load_terms = pltpu.make_async_copy(terms_hbm, terms, load_sem.at[0])
    load_base = pltpu.make_async_copy(base_hbm, base, load_sem.at[1])
    load_blocks = pltpu.make_async_copy(blocks_hbm, blocks, load_sem.at[2])
    load_owner = pltpu.make_async_copy(owner_hbm, owner_ref, load_sem.at[3])
    load_slot = pltpu.make_async_copy(slot_hbm, slot_ref, load_sem.at[4])
    load_cols = pltpu.make_async_copy(cols_hbm, cols_ref, load_sem.at[5])
    for load in (load_owner, load_slot, load_terms, load_base, load_cols, load_blocks):
        load.start()

    barrier = pltpu.get_barrier_semaphore()

    @pl.loop(1, n)
    def _(step):
        pl.semaphore_signal(barrier, inc=1, device_id={"row": (me + step) % n}, device_id_type=MESH)

    load_owner.wait()
    owner = owner_ref[...]
    matches = (lax.broadcasted_iota(jnp.int32, (n, count), 0) == owner).astype(F32)
    before = lax.broadcasted_iota(jnp.int32, (count, count), 0) < lax.broadcasted_iota(jnp.int32, (count, count), 1)
    earlier = jnp.dot(matches.astype(BF16), before.astype(F32).astype(BF16), preferred_element_type=F32)
    order_in = jnp.sum(earlier * matches, axis=0, keepdims=True).astype(jnp.int32)
    position = ((owner // 2) % 2 * (n // 2) + owner // 4 * 2 + owner % 2) * cap + order_in
    picker = (lax.broadcasted_iota(jnp.int32, (n * cap, count), 0) == position).astype(F32).astype(BF16)

    def slot_of(device):
        return (device // 2) % 2 * (n // 2) + device // 4 * 2 + device % 2

    def tag_copy(peer, source):
        return pltpu.make_async_remote_copy(
            src_ref=tags_out.at[peer], dst_ref=tags_in.at[source], send_sem=tag_sem.at[0],
            recv_sem=tag_sem.at[1], device_id={"row": peer}, device_id_type=MESH)

    def row_copy(j, peer, source):
        return pltpu.make_async_remote_copy(
            src_ref=outgoing[j].at[slot_of(peer)], dst_ref=arrived[j].at[source], send_sem=a2a_send.at[j],
            recv_sem=a2a_recv.at[j], device_id={"row": peer}, device_id_type=MESH)

    def all_tags():
        others = pl.ds(0, n - 1)
        return pltpu.make_async_remote_copy(
            src_ref=tags_out.at[others], dst_ref=tags_in.at[others], send_sem=tag_sem.at[0],
            recv_sem=tag_sem.at[1], device_id={"row": (me + 1) % n}, device_id_type=MESH)

    def all_rows(j):
        others = pl.ds(0, n - 1)
        return pltpu.make_async_remote_copy(
            src_ref=outgoing[j].at[others], dst_ref=arrived[j].at[others], send_sem=a2a_send.at[j],
            recv_sem=a2a_recv.at[j], device_id={"row": (me + 1) % n}, device_id_type=MESH)

    own_tags = pltpu.make_async_copy(tags_out.at[me], tags_in.at[me], own_sem.at[CHUNKS])
    own_rows = [
        pltpu.make_async_copy(outgoing[j].at[slot_of(me)], arrived[j].at[me], own_sem.at[j]) for j in range(CHUNKS)
    ]

    def pack(j):
        sent = jnp.dot(picker, terms[:, starts[j]:starts[j] + wides[j]], preferred_element_type=F32)
        outgoing[j][...] = sent.astype(BF16).reshape(outgoing[j].shape)

    my_z, y_peer = me // 4, me + 2 * sign_y

    def over_y(j, hop):
        first = slot_of(me + 2 * sign_y + 4 * hop * sign_y - me % 2)
        return pltpu.make_async_remote_copy(
            src_ref=outgoing[j].at[pl.ds(first, 2)], dst_ref=passing[j].at[hop - 1], send_sem=a2a_send.at[j],
            recv_sem=pass_recv.at[j, hop - 1], device_id={"row": y_peer}, device_id_type=MESH)

    def over_z(j, hop, core):
        return pltpu.make_async_remote_copy(
            src_ref=passing[j].at[hop - 1, core], dst_ref=arrived[j].at[y_peer],
            send_sem=pass_send.at[j, hop - 1], recv_sem=a2a_recv.at[j],
            device_id={"row": me - me % 2 + core - 4 * hop * sign_y}, device_id_type=MESH)

    def passed(j, hop):
        return pltpu.make_async_remote_copy(
            src_ref=passing[j].at[hop - 1], dst_ref=passing[j].at[hop - 1], send_sem=pass_send.at[j, hop - 1],
            recv_sem=pass_recv.at[j, hop - 1], device_id={"row": y_peer}, device_id_type=MESH)

    def plane(there):
        return jnp.logical_and(there >= 0, there < n // 4)

    def straight(hop, behind):
        return jnp.logical_and(EDGE and hop == 2, jnp.logical_and(me % 2 == 1, jnp.logical_not(plane(behind))))

    def goes_over(hop):
        return jnp.logical_and(plane(my_z + hop * sign_y), jnp.logical_not(straight(hop, my_z - sign_y)))

    def comes_over(hop):
        return jnp.logical_and(plane(my_z - hop * sign_y), jnp.logical_not(straight(hop, my_z + sign_y)))

    def pass_rows(j):
        for hop in RELAYED[j]:
            @pl.when(comes_over(hop))
            def _(hop=hop):
                passed(j, hop).wait_recv()
                for core in range(2):
                    over_z(j, hop, core).start()

    def send_over(j):
        for hop in reversed(RELAYED[j]):
            @pl.when(goes_over(hop))
            def _(hop=hop):
                over_y(j, hop).start()

    def send_rows(j):
        @pl.loop(1, n)
        def _(step):
            peer = (me + step) % n
            hops = (peer // 4 - my_z) * sign_y
            other_y = (peer // 2) % 2 != (me // 2) % 2
            over = jnp.bool_(False)
            for hop in RELAYED[j]:
                over = jnp.logical_or(over, jnp.logical_and(hops == hop, goes_over(hop)))
            over = jnp.logical_and(other_y, over)

            @pl.when(jnp.logical_not(over))
            def _():
                row_copy(j, peer, me).start()

        own_rows[j].start()

    load_terms.wait()
    for j in range(CHUNKS):
        pack(j)
    per_row = LANES // cap
    lane_of = order_in + (me % per_row) * cap
    lanes = (lax.broadcasted_iota(jnp.int32, (LANES, count), 0) == lane_of).astype(F32).astype(BF16)
    load_slot.wait()
    tag = slot_ref[...] + 1
    high = (tag // 32).astype(F32)
    low = (tag % 32).astype(F32)
    over_rows = (((1,), (1,)), ((), ()))
    tags = 32.0 * lax.dot_general((matches * high).astype(BF16), lanes, over_rows, preferred_element_type=F32)
    tags = tags + lax.dot_general((matches * low).astype(BF16), lanes, over_rows, preferred_element_type=F32)
    tags = tags.astype(jnp.int32)
    for peer in range(n):
        tags_out[peer] = jnp.broadcast_to(tags[peer:peer + 1], tags_out.shape[1:])

    pl.semaphore_wait(barrier, n - 1)

    @pl.loop(1, n)
    def _(step):
        tag_copy((me + step) % n, me).start()

    own_tags.start()

    for j in SENDS[0]:
        send_over(j)
        send_rows(j)
    for j in SENDS[0]:
        pass_rows(j)
    for j in range(CHUNKS):
        if j not in SENDS[0]:
            send_over(j)
    all_tags().wait_recv()
    own_tags.wait()
    packed = []
    for first in range(0, n, per_row):
        total = tags_in[first][0:1]
        for source in range(first + 1, min(first + per_row, n)):
            total = total + tags_in[source][0:1]
        packed.append(total)
    arrived_tags = jnp.concatenate(packed, axis=1) - 1
    tall = seg_dev // 4
    for part in range(4):
        seg_ids = lax.broadcasted_iota(jnp.int32, (tall, n * cap), 0) + part * tall
        landing[part * tall:(part + 1) * tall] = (seg_ids == arrived_tags).astype(F32).astype(BF16)
    load_base.wait()

    def halo_copy(kind, j, from_slot, to_slot, peer):
        return pltpu.make_async_remote_copy(
            src_ref=windows[j].at[pl.ds(rows_dev * from_slot, rows_dev)],
            dst_ref=windows[j].at[pl.ds(rows_dev * to_slot, rows_dev)],
            send_sem=halo_send.at[kind, j], recv_sem=halo_recv.at[kind, j],
            device_id={"row": peer}, device_id_type=MESH)

    def piece_copy(kind, p, from_slot, to_slot, peer):
        j, q = divmod(p, rows_dev)
        recv_sem = halo_recv.at[kind, j] if kind == TO_RELAY else piece_recv.at[kind, p]
        return pltpu.make_async_remote_copy(
            src_ref=windows[j].at[rows_dev * from_slot + q], dst_ref=windows[j].at[rows_dev * to_slot + q],
            send_sem=halo_send.at[kind, j], recv_sem=recv_sem, device_id={"row": peer}, device_id_type=MESH)

    y_way = (HALO, HALO - 2 * sign_y, me + 2 * sign_y)
    core_way = (HALO, HALO - sign_c, me + sign_c)
    z_way = (HALO + 2 * sign_y, HALO - 2 * sign_y, z_to)
    relay_way = (HALO + 2 * sign_c, HALO + sign_c, me + sign_c)
    relay_sends = jnp.logical_or(sign_y == sign_c, z_comes)
    relay_comes = jnp.logical_or(sign_y != sign_c, z_comes)
    first_block = (me - HALO) * rows_dev
    pieces = CHUNKS * rows_dev

    def own(j):
        all_rows(j).wait_recv()
        own_rows[j].wait()
        for i in SENDS[j + 1] if j + 1 < len(SENDS) else ():
            send_rows(i)
            pass_rows(i)
        rows = arrived[j][...].reshape(n * cap, wides[j])
        for q in range(rows_dev):
            place = slice(q * block, (q + 1) * block)
            injected = jnp.dot(landing[place], rows, preferred_element_type=F32)
            before_it = base[place, starts[j]:starts[j] + wides[j]].astype(F32)
            windows[j][HALO * rows_dev + q] = (before_it + injected).astype(BF16)
        halo_copy(TO_CORE, j, *core_way).start()

    def y_arrives(p):
        slot = HALO + 2 * sign_y
        piece_copy(TO_Y, p, slot, slot, me + 2 * sign_y).wait_recv()

        @pl.when(z_sends)
        def _():
            piece_copy(TO_Z, p, *z_way).start()

        @pl.when(sign_y == sign_c)
        def _():
            piece_copy(TO_RELAY, p, *relay_way).start()

    def z_arrives(p):
        slot = HALO - 2 * sign_y

        @pl.when(z_comes)
        def _():
            piece_copy(TO_Z, p, slot, slot, me + 2 * sign_y).wait_recv()

        @pl.when(jnp.logical_and(z_comes, sign_y != sign_c))
        def _():
            piece_copy(TO_RELAY, p, *relay_way).start()

    def window_complete(j):
        halo_copy(TO_CORE, j, HALO + sign_c, HALO + sign_c, me + sign_c).wait_recv()

        @pl.when(relay_comes)
        def _():
            halo_copy(TO_RELAY, j, HALO - sign_c, HALO - sign_c, me + sign_c).wait_recv()

    def compute(j, r):
        total = jnp.zeros((block, wides[j]), F32)
        for k in range(stored):
            place = jnp.clip(cols_ref[r, k] - first_block, 0, windows[j].shape[0] - 1)
            total = total + jnp.dot(blocks[r, k], windows[j][place], preferred_element_type=F32)
        out_ref[r * block:(r + 1) * block, starts[j]:starts[j] + wides[j]] = total.astype(BF16)

    own(0)
    for p in range(rows_dev):
        piece_copy(TO_Y, p, *y_way).start()
    upcoming = rows_dev
    z_lag = Z_LAG
    first_compute = min(LAGS)
    for p in range(pieces - rows_dev + max(LAGS) + 1):
        if p < pieces:
            y_arrives(p)
            while upcoming < pieces and upcoming - p <= DEPTHS[upcoming // rows_dev]:
                if upcoming % rows_dev == 0:
                    own(upcoming // rows_dev)
                piece_copy(TO_Y, upcoming, *y_way).start()
                upcoming += 1
        if 0 <= p - z_lag < pieces:
            z_arrives(p - z_lag)
        if p == first_compute:
            load_cols.wait()
            load_blocks.wait()
        for j in range(CHUNKS):
            for r in range(rows_dev):
                if p == rows_dev * j + LAGS[r % len(LAGS)]:
                    if r == 0:
                        window_complete(j)
                    compute(j, r)

    all_tags().wait_send()
    for j in range(CHUNKS):
        all_rows(j).wait_send()
        halo_copy(TO_Y, j, *y_way).wait_send()
        halo_copy(TO_CORE, j, *core_way).wait_send()

        @pl.when(z_sends)
        def _():
            halo_copy(TO_Z, j, *z_way).wait_send()

        @pl.when(relay_sends)
        def _():
            halo_copy(TO_RELAY, j, *relay_way).wait_send()

        for hop in RELAYED[j]:
            @pl.when(comes_over(hop))
            def _(hop=hop):
                passed(j, hop).wait_send()


def shards(base_currents, term_rows, term_owner, term_slot, inductance, block_cols):
    n = lax.axis_size("row")
    seg_dev, width = base_currents.shape
    count = term_rows.shape[0]
    rows_dev, stored, block, _ = inductance.shape
    cap = max(16, 2 * count // n)
    wides = [width * part // sum(WIDTHS) for part in WIDTHS]
    span = (2 * HALO + 1) * rows_dev
    hbm = pl.BlockSpec(memory_space=pltpu.HBM)
    dma = pltpu.SemaphoreType.DMA
    return pl.pallas_call(
        functools.partial(kernel, n, cap),
        out_shape=pltpu.VMEM((seg_dev, width), BF16),
        in_specs=[hbm] * 6,
        out_specs=pl.BlockSpec(memory_space=pltpu.VMEM),
        scratch_shapes=(
            [pltpu.VMEM((span, block, wide), BF16) for wide in wides]
            + [pltpu.VMEM((n, cap, wide), BF16) for wide in wides]
            + [pltpu.VMEM((n, cap, wide), BF16) for wide in wides]
            + [pltpu.VMEM((2, 2, cap, wide), BF16) for wide in wides]
            + [
                pltpu.SMEM(block_cols.shape, jnp.int32),
                pltpu.VMEM((1, count), jnp.int32),
                pltpu.VMEM((1, count), jnp.int32),
                pltpu.VMEM((count, width), BF16),
                pltpu.VMEM((seg_dev, width), BF16),
                pltpu.VMEM(inductance.shape, BF16),
                pltpu.VMEM((seg_dev, n * cap), BF16),
                pltpu.VMEM((n, 8, LANES), jnp.int32),
                pltpu.VMEM((n, 8, LANES), jnp.int32),
                dma((6,)),
                dma((CHUNKS + 1,)),
                dma((CHUNKS,)),
                dma((CHUNKS,)),
                dma((CHUNKS, 2)),
                dma((CHUNKS, 2)),
                dma((2,)),
                dma((4, CHUNKS)),
                dma((4, CHUNKS)),
                dma((2, CHUNKS * rows_dev)),
            ]
        ),
        compiler_params=pltpu.CompilerParams(
            collective_id=0, has_side_effects=True, vmem_limit_bytes=48 * 2**20
        ),
        cost_estimate=pl.CostEstimate(
            flops=2 * rows_dev * stored * block * block * width,
            bytes_accessed=2 * (inductance.size + 2 * base_currents.size + term_rows.size),
            transcendentals=0,
        ),
    )(*[
        pltpu.with_memory_space_constraint(array, pltpu.HBM)
        for array in (
            block_cols, term_owner.reshape(1, count), term_slot.reshape(1, count), term_rows, base_currents, inductance
        )
    ])


def solution(mesh):
    placed = (
        P(("group", "row"), None),
        P(("group", "row"), None),
        P(("group", "row"), None),
        P(("group", "row"), None),
        P("row", None, None, None),
        P("row", None),
    )
    return jax.shard_map(
        shards, mesh=mesh, in_specs=placed, out_specs=P(("group", "row"), None), check_vma=False
    )
```
